32 devices in a mesh: seq: 8 (over z, x), head: 4 (over y, core).
Axes of the slice: x: 2, y: 2, z: 4, core: 2. Of those that a mesh axis runs over, the one named last changes fastest.
Arguments:
- queries: bfloat16 [4, 64, 64, 128], P(None, 'seq', 'head')
- new_kv: bfloat16 [2, 4, 64, 8, 128], P(None, None, 'seq', 'head'), may hold values from -12 to 12
- prompt_keys: bfloat16 [8, 8192, 8, 128], P(None, 'seq', 'head')
- prompt_values: bfloat16 [8, 8192, 8, 128], P(None, 'seq', 'head'), may hold values from -6 to 6
- suffix_kv: bfloat16 [2, 64, 512, 8, 128], P(None, 'seq', None, 'head'), may hold values from -9.5625 to 9.5625
- prompt_ids: int32 [64, 1], P('seq'), may hold values from 0 to 7
- suffix_lengths: int32 [64], P('seq'), may hold values from 1 to 512, 16384 in all
- token_ids: int32 [64, 4], replicated, may hold values from 0 to 65535
- embedding: bfloat16 [65536, 8192], P('head', 'seq'), may hold values from -3 to 3
- out_weight: bfloat16 [8192, 8192], P('head', 'seq'), may hold values from -0.25 to 0.25
Outputs:
- hidden_out: bfloat16 [64, 4, 8192], P('head', None, 'seq')
The draws below stay inside these ranges and needn't reach their ends.
Inputs may be any that keep to these rules, and one draw needn't show every extreme that they name: `prompt_ids`: every one of the 8 prompts is named by some row.
All inputs are finite; a program needn't handle non-finite values. No bound on the sum of `suffix_lengths` on one device may be relied on, other than what follows from the above.
Results may differ from the reference program's by a relative error of at most 0.02.
Values may be sent and summed in bfloat16 or wider, within the bound.
A program may use at most 320 MiB of HBM per device.

```python
import math
import jax
import jax.numpy as jnp
import numpy as np
from jax import lax

D = 8192
H = 64
KVH = 8
HD = 128
VOCAB = 65536
STEPS = 4
PROMPTS = 8
SUF = 512
ROWS = 64
PLEN = 8192


def draw_queries(key, part):
    values = 2.5 * jax.random.normal(jax.random.fold_in(key, 11), (STEPS, ROWS, H, HD), jnp.float32)
    values = jnp.clip(values, -15.0, 15.0)
    return values.astype(jnp.bfloat16)


def draw_prompt_keys(key, part):
    values = jax.random.normal(jax.random.fold_in(key, 12), (PROMPTS, PLEN, KVH, HD), jnp.float32)
    values = jnp.clip(values, -6.0, 6.0)
    return values.astype(jnp.bfloat16)


def place_ends(array, own_key, low, high):
    dims = array.shape
    index_at = [jax.random.randint(jax.random.fold_in(own_key, axis), (), 0, dims[axis]) for axis in range(len(dims))]
    array = array.at[tuple(index_at)].set(low)
    longest = dims.index(max(dims))
    index_at[longest] = (index_at[longest] + 1) % dims[longest]
    return array.at[tuple(index_at)].set(high)


def levels(stream_key, extent, cuts, least, largest):
    def one(dim, shards_of):
        draws = jax.random.uniform(jax.random.fold_in(jax.random.fold_in(stream_key, 6), dim), (shards_of,), jnp.float32, least / len(cuts), largest / len(cuts))
        return jnp.repeat(jnp.exp(draws), extent[dim] // shards_of).reshape((-1,) + (1,) * (len(extent) - dim - 1))

    gain = one(*cuts[0])
    for cut in cuts[1:]:
        gain = gain * one(*cut)
    return gain


def rank_table(number_of, lean):
    weights = [(1 << 20) // math.isqrt(grade ** lean) + 1 for grade in range(1, number_of + 1)]
    scale = 1 + sum(weights) // (1 << 30)
    return np.cumsum(np.array([max(1, weight // scale) for weight in weights]))


def ranked_ids(key, extent, count, lean):
    grid = rank_table(count, lean)
    pick = jax.random.randint(jax.random.fold_in(key, 1), extent, 0, int(grid[count - 1]))
    standing = jnp.searchsorted(jnp.asarray(grid, jnp.int32), pick, side="right")
    return jax.random.permutation(jax.random.fold_in(key, 2), count)[standing].astype(jnp.int32)


def different_ones(own_key, rows, number_of, top, lift):
    ranking = jax.random.permutation(jax.random.fold_in(own_key, 1), number_of)
    favour = ranking
    for power in range(3):
        favour = favour * favour // number_of
    favour = favour * lift // number_of
    chance = jax.random.randint(jax.random.fold_in(own_key, 2), (rows, number_of), 0, 4096) + favour
    holders = jax.random.permutation(jax.random.fold_in(own_key, 3), rows)[jnp.arange(number_of) % rows]
    chance = jnp.where(jnp.arange(rows)[:, None] == holders[None, :], 1 << 14, chance)
    merit = chance * number_of + jnp.arange(number_of)
    return lax.top_k(merit.astype(jnp.int32), top)[1].astype(jnp.int32)


def length_profile(amount, total, most, lean):
    weights = [(1 << 20) // math.isqrt(grade ** lean) + 1 for grade in range(2, amount + 1)]
    spare, holding = total - most - (amount - 1), [1] * (amount - 1)
    while spare > 0:
        candidates = [i for i in range(amount - 1) if holding[i] < most]
        pool, left = sum([weights[i] for i in candidates]), spare
        for i in candidates:
            extra = min(most - holding[i], max(1, left * weights[i] // pool), spare)
            holding[i] = holding[i] + extra
            spare = spare - extra
    return np.array([most] + holding)


def uneven_parts(key, count, total, limit, slope):
    if count == 2:
        one = jax.random.randint(key, (), max(1, total - limit), min(limit, total - 1) + 1)
        return jnp.stack([one, total - one])
    lengths = jnp.asarray(length_profile(count, total, limit, slope), jnp.int32)
    pairs = (count - 1) // 2
    source_of, sink = lengths[1:1 + 2 * pairs:2], lengths[2:2 + 2 * pairs:2]
    slack = jnp.minimum(source_of - 1, limit - sink)
    shifted = jax.random.randint(jax.random.fold_in(key, 1), (pairs,), 0, 1 << 20) % (slack + 1)
    lengths = lengths.at[1:1 + 2 * pairs:2].set(source_of - shifted).at[2:2 + 2 * pairs:2].set(sink + shifted)
    return lengths[jax.random.permutation(jax.random.fold_in(key, 2), count)]


def bell_draw(rng, extent, deviation, most, cuts=(), held_as=jnp.bfloat16):
    values = deviation * jax.random.normal(rng, extent, jnp.float32)
    if cuts:
        values = values * levels(rng, extent, cuts, -0.22, 0.18)
    return jnp.clip(values, -most, most).astype(held_as)


def setup_inputs(seed: int = 0) -> dict:
    keys = jax.random.split(jax.random.key(seed), 11)
    return {
        "queries": draw_queries(jax.random.fold_in(keys[10], 71), 0),
        "new_kv": bell_draw(keys[1], (2, STEPS, ROWS, KVH, HD), 2.0, 12.0, ((2, 8), (3, 4))),
        "prompt_keys": draw_prompt_keys(jax.random.fold_in(keys[10], 71), 0),
        "prompt_values": bell_draw(keys[3], (PROMPTS, PLEN, KVH, HD), 1.0, 6.0, ((1, 8), (2, 4))),
        "suffix_kv": bell_draw(keys[4], (2, ROWS, SUF, KVH, HD), 1.6, 9.5625, ((1, 8), (3, 4))),
        "prompt_ids": different_ones(keys[5], ROWS, PROMPTS, 1, 1024),
        "suffix_lengths": uneven_parts(keys[6], ROWS, ROWS * SUF // 2, SUF, 2).astype(jnp.int32),
        "token_ids": place_ends(ranked_ids(keys[7], (ROWS, STEPS), VOCAB, 2), jax.random.fold_in(keys[7], 3), 0, VOCAB - 1).astype(jnp.int32),
        "embedding": bell_draw(keys[8], (VOCAB, D), 0.5, 3.0, ((0, 4), (1, 8))),
        "out_weight": bell_draw(keys[9], (H * HD, D), (4 * HD) ** -0.5, 0.25, ((0, 4), (1, 8))),
    }


def rounded(weights):
    return lax.optimization_barrier(weights.astype(jnp.bfloat16)).astype(jnp.float32)


def reference(queries, new_kv, prompt_keys, prompt_values, suffix_kv, prompt_ids, suffix_lengths, token_ids, embedding, out_weight):
    group_size = H // KVH
    score_scale = HD ** -0.5
    live_pos = jnp.arange(SUF, dtype=jnp.int32)
    step_order = jnp.arange(STEPS, dtype=jnp.int32)
    causal = step_order[None, :] <= step_order[:, None]
    row_queries = jnp.moveaxis(queries, 1, 0)
    row_fresh = jnp.moveaxis(new_kv, 2, 0)
    row_suffix = jnp.moveaxis(suffix_kv, 1, 0)

    def one_row(inputs):
        query_rows, fresh_rows, suffix, prompt_row, length = inputs
        query_f = query_rows.astype(jnp.float32).reshape(STEPS, KVH, group_size, HD)
        prompt_key = prompt_keys[prompt_row].astype(jnp.float32)
        prompt_val = prompt_values[prompt_row].astype(jnp.float32)
        score_prompt = jnp.einsum("tcgd,kcd->ctgk", query_f, prompt_key) * score_scale
        score_suffix = jnp.einsum("tcgd,kcd->ctgk", query_f, suffix[0].astype(jnp.float32)) * score_scale
        live_mask = (live_pos < length)[None, None, None, :]
        score_suffix = jnp.where(live_mask, score_suffix, -jnp.inf)
        score_fresh = jnp.einsum("tcgd,ucd->ctgu", query_f, fresh_rows[0].astype(jnp.float32)) * score_scale
        score_fresh = jnp.where(causal[None, :, None, :], score_fresh, -jnp.inf)
        highest = jnp.maximum(jnp.max(score_prompt, axis=-1), jnp.maximum(jnp.max(score_suffix, axis=-1), jnp.max(score_fresh, axis=-1)))
        weight_prompt = jnp.exp(score_prompt - highest[..., None])
        weight_suffix = jnp.exp(score_suffix - highest[..., None])
        weight_fresh = jnp.exp(score_fresh - highest[..., None])
        denominator = jnp.sum(weight_prompt, axis=-1) + jnp.sum(weight_suffix, axis=-1) + jnp.sum(weight_fresh, axis=-1)
        blended = jnp.einsum("ctgk,kcd->ctgd", rounded(weight_prompt), prompt_val)
        blended = blended + jnp.einsum("ctgk,kcd->ctgd", rounded(weight_suffix), suffix[1].astype(jnp.float32))
        blended = blended + jnp.einsum("ctgu,ucd->ctgd", rounded(weight_fresh), fresh_rows[1].astype(jnp.float32))
        return (blended / denominator[..., None]).astype(jnp.bfloat16)

    attention = lax.map(one_row, (row_queries, row_fresh, row_suffix, prompt_ids[:, 0].astype(jnp.int32), suffix_lengths.astype(jnp.int32)))
    weight_full = out_weight.astype(jnp.float32).reshape(KVH, group_size, HD, D)
    projected = jnp.einsum("rctgd,cgde->rte", attention.astype(jnp.float32), weight_full)
    embedded = jnp.take(embedding, token_ids, axis=0).astype(jnp.float32)
    return (projected + embedded).astype(jnp.bfloat16)
```

```python
import functools
import math

import jax
import jax.numpy as jnp
from jax import lax
from jax.experimental import pallas as pl
from jax.experimental.pallas import tpu as pltpu
from jax.sharding import PartitionSpec as P

MESH = pl.DeviceIdType.MESH
F32 = jnp.float32
BF16 = jnp.bfloat16
NT = (((1,), (1,)), ((), ()))
VMEM_BYTES = 58 * 2**20


def split_axis(n):
    inner = 2 if n <= 8 else 8
    return n // inner, inner


def greet(peers):
    barrier = pltpu.get_barrier_semaphore()
    for peer in peers:
        pl.semaphore_signal(barrier, inc=1, device_id=peer, device_id_type=MESH)
    pl.semaphore_wait(barrier, len(peers))


def seq_peers(n, me):
    outer, inner = split_axis(n)
    a, b = me // inner, lax.rem(me, inner)
    line = [lax.rem(a + k, outer) * inner + b for k in range(outer)]
    side = [a * inner + lax.rem(b + j, inner) for j in range(inner)]
    return line, side


class Gather:
    def __init__(self, n, me, bufs, send1, recv1, send2, recv2):
        self.n, self.me, self.bufs = n, me, bufs
        self.outer, self.inner = split_axis(n)
        self.sems = (send1, recv1, send2, recv2)
        self.a, self.b = me // self.inner, lax.rem(me, self.inner)
        self.sent = []

    def shard(self, k, j):
        a = lax.rem(self.a - k + self.outer, self.outer)
        b = lax.rem(self.b - j + self.inner, self.inner)
        return a * self.inner + b

    def copy1(self, i, k, shard):
        send1, recv1, _, _ = self.sems
        peer = lax.rem(self.a + k, self.outer) * self.inner + self.b
        buf = self.bufs[i]
        return pltpu.make_async_remote_copy(
            src_ref=buf.at[shard], dst_ref=buf.at[shard], send_sem=send1.at[i, k], recv_sem=recv1.at[i, k],
            device_id={"seq": peer}, device_id_type=MESH)

    def copy2(self, i, k, j, shard):
        _, _, send2, recv2 = self.sems
        peer = self.a * self.inner + lax.rem(self.b + j, self.inner)
        buf = self.bufs[i]
        return pltpu.make_async_remote_copy(
            src_ref=buf.at[shard], dst_ref=buf.at[shard], send_sem=send2.at[i, k, j], recv_sem=recv2.at[i, k, j],
            device_id={"seq": peer}, device_id_type=MESH)

    def begin(self, copy):
        copy.start()
        self.sent.append(copy)

    def start(self):
        for k in range(1, self.outer):
            for i in range(len(self.bufs)):
                self.begin(self.copy1(i, k, self.me))
        self.forward(0)

    def forward(self, k):
        shard = self.shard(k, 0)
        for i in range(len(self.bufs)):
            if k:
                self.copy1(i, k, shard).wait_recv()
            for j in range(1, self.inner):
                self.begin(self.copy2(i, k, j, shard))

    def finish(self):
        for k in range(self.outer):
            for j in range(1, self.inner):
                for i in range(len(self.bufs)):
                    self.copy2(i, k, j, self.shard(k, j)).wait_recv()
        for copy in self.sent:
            copy.wait_send()


def gather_sems(n, count):
    outer, inner = split_axis(n)
    line = pltpu.SemaphoreType.DMA((count, outer))
    side = pltpu.SemaphoreType.DMA((count, outer, inner))
    return [line, line, side, side]


def eye(rows, lanes=128):
    return lax.broadcasted_iota(jnp.int32, (rows, lanes), 0) == lax.broadcasted_iota(jnp.int32, (rows, lanes), 1)


def to_row(column):
    return jnp.sum(jnp.where(eye(column.shape[0]), column, 0.0), axis=0, keepdims=True)


def to_column(row, rows):
    return jnp.sum(jnp.where(eye(rows), row, 0.0), axis=1, keepdims=True)


def softmax_mix(scores, values, scale2):
    peak = jnp.max(scores, axis=-1, keepdims=True)
    weights = jnp.exp2((scores - peak) * scale2)
    total = jnp.sum(weights, axis=-1, keepdims=True)
    mixed = jnp.dot(weights.astype(BF16), values, preferred_element_type=F32)
    return mixed / total, peak * scale2 + jnp.log2(total)


def share_kernel(n, scale2, steps, lengths, q_own, ids_own, fresh, suffix, q_all, ids_all, mixed_ref, lse_ref,
                 raw, wide, keys, values, local_sem, send1, recv1, send2, recv2):
    rows, kv, queries, width = q_own.shape
    suf = suffix.shape[2] // kv
    live = keys.shape[1]
    me = lax.axis_index("seq")
    line, side = seq_peers(n, me)
    greet([{"seq": d} for d in line[1:] + side[1:]])
    q_all[me] = q_own[...]
    ids_all[me] = ids_own[...]
    gather = Gather(n, me, [q_all, ids_all], send1, recv1, send2, recv2)
    gather.start()
    load = pltpu.make_async_copy(suffix, raw, local_sem.at[0])
    load.start()
    keys[...] = jnp.zeros_like(keys)
    values[...] = jnp.zeros_like(values)
    column = lax.broadcasted_iota(jnp.int32, (queries, live), 1)
    step = lax.broadcasted_iota(jnp.int32, (queries, live), 0) // (queries // steps)
    new = jnp.logical_and(column >= suf, column - suf <= step)
    load.wait()

    def one_row(r, carry):
        old = column < lengths[r]
        stats = []
        for part, store in ((0, keys), (1, values)):
            wide[part] = raw[part, r].astype(F32)
            for c in range(kv):
                store[c, 0:suf] = wide[part, pl.ds(c, suf, stride=kv), :].astype(BF16)
                store[c, suf:suf + fresh.shape[3]] = fresh[part, r, c]
        for c in range(kv):
            scores = lax.dot_general(q_own[r, c], keys[c], NT, preferred_element_type=F32)
            scores = jnp.where(jnp.logical_or(old, new), scores, -jnp.inf)
            mixed, lse = softmax_mix(scores, values[c], scale2)
            mixed_ref[r, c * queries:(c + 1) * queries] = mixed
            stats.append(lse)
        lse_ref[pl.ds(r, 1), :] = to_row(jnp.concatenate(stats, axis=0))
        return carry

    outer = gather.outer
    for k in range(outer):
        lax.fori_loop(rows * k // outer, rows * (k + 1) // outer, one_row, 0)
        if k + 1 < outer:
            gather.forward(k + 1)
    gather.finish()


def prompt_kernel(scale2, tile, ids, local_ids, q_ref, k_ref, v_ref, rem_ref, embedding, o_ref, lse_ref, e_ref,
                  order, wide, keys, values, blocks, sem):
    p = pl.program_id(0)
    rows, kv, queries, width = q_ref.shape
    positions = k_ref.shape[1] // kv
    vocab = embedding.shape[0]
    tokens = rem_ref.shape[0]

    @pl.when(p == 0)
    def _():
        def fetch(i, carry):
            first = pl.multiple_of(jnp.clip(local_ids[i], 0, vocab - 1) // 16 * 16, 16)
            pltpu.make_async_copy(embedding.at[pl.ds(first, 16)], blocks.at[pl.ds(pl.multiple_of(i * 16, 16), 16)], sem.at[0]).start()
            return carry
        lax.fori_loop(0, tokens, fetch, 0)

    def scan(r, count):
        order[count] = r
        return count + (ids[r] == p).astype(jnp.int32)

    count = lax.fori_loop(0, rows, scan, 0)
    last = order[jnp.maximum(count - 1, 0)]
    for j in range(tile):
        order[count + j] = last
    for source, store, part in ((k_ref, keys, 0), (v_ref, values, 1)):
        wide[part] = source[0].astype(F32)
        for c in range(kv):
            store[c] = wide[part, pl.ds(c, positions, stride=kv), :].astype(BF16)

    def one_tile(i, carry):
        picked = [order[i * tile + j] for j in range(tile)]
        results = []
        for c in range(kv):
            query = jnp.concatenate([q_ref[r, c] for r in picked], axis=0)
            scores = lax.dot_general(query, keys[c], NT, preferred_element_type=F32)
            results.append(softmax_mix(scores, values[c], scale2))
        for j, r in enumerate(picked):
            span = slice(j * queries, (j + 1) * queries)
            for c in range(kv):
                o_ref[r, c * queries:(c + 1) * queries] = results[c][0][span].astype(BF16)
            lse_ref[pl.ds(r, 1), :] = to_row(jnp.concatenate([results[c][1][span] for c in range(kv)], axis=0))
        return carry

    lax.fori_loop(0, (count + tile - 1) // tile, one_tile, 0)

    @pl.when(p == pl.num_programs(0) - 1)
    def _():
        span = min(vocab, tokens * 16)
        for i in range(tokens * 16 // span):
            pltpu.make_async_copy(embedding.at[pl.ds(0, span)], blocks.at[pl.ds(i * span, span)], sem.at[0]).wait()
        lane = lax.broadcasted_iota(jnp.int32, (16, 256), 1)
        owner = lane // 16 == lax.broadcasted_iota(jnp.int32, (16, 256), 0)

        def pick(i, carry):
            rem = rem_ref[pl.ds(pl.multiple_of(i * 16, 16), 16), 0:1]
            chosen = jnp.logical_and(owner, lax.rem(lane, 16) == rem).astype(F32).astype(BF16)
            block = blocks[pl.ds(pl.multiple_of(i * 256, 256), 256), :]
            e_ref[pl.ds(pl.multiple_of(i * 16, 16), 16), :] = jnp.dot(chosen, block, preferred_element_type=F32).astype(BF16)
            return carry
        lax.fori_loop(0, tokens // 16, pick, 0)


def finish_kernel(n, heads_n, steps, kv, o_ref, lse_ref, s_ref, s_lse, e_ref, weight, out_ref,
                  side_o, side_l, line_o, line_l, pass_o, pass_l, share, flat, att_all, w_buf, part, landed,
                  local_sem, so1, ro1, sl1, rl1, so2, ro2, sl2, rl2, gs1, gr1, gs2, gr2, hs, hr):
    rows, queries, width = s_ref.shape
    outer, inner = split_axis(n)
    me = lax.axis_index("seq")
    head = lax.axis_index("head")
    line, side = seq_peers(n, me)
    a, b = me // inner, lax.rem(me, inner)
    load = pltpu.make_async_copy(weight, w_buf, local_sem.at[0])
    load.start()
    greet([{"seq": d} for d in line[1:] + side[1:]] + [{"head": lax.rem(head + i, heads_n)} for i in range(1, heads_n)])
    order = list(range(1, outer)) + [0]

    def remote(src, dst, send, recv, **to):
        return pltpu.make_async_remote_copy(src_ref=src, dst_ref=dst, send_sem=send, recv_sem=recv, device_id=to, device_id_type=MESH)

    def side_copies(k, j):
        shard = lax.rem(a + k, outer) * inner + lax.rem(b + j, inner)
        return [remote(o_ref.at[shard], side_o.at[k, j], so1.at[k, j], ro1.at[k, j], seq=side[j]),
                remote(lse_ref.at[shard], side_l.at[k, j], sl1.at[k, j], rl1.at[k, j], seq=side[j])]

    def line_copies(k):
        return [remote(pass_o.at[k], line_o.at[k], so2.at[k], ro2.at[k], seq=line[k]),
                remote(pass_l.at[k], line_l.at[k], sl2.at[k], rl2.at[k], seq=line[k])]

    sent = []
    for k in order:
        for j in range(1, inner):
            for copy in side_copies(k, j):
                copy.start()
                sent.append(copy)

    def blend(lses, read, write):
        peak = functools.reduce(jnp.maximum, lses)
        raw = [jnp.exp2(l - peak) for l in lses]
        total = functools.reduce(jnp.add, raw)
        for i, w in enumerate(raw):
            share[i] = w / total

        def one_row(r, carry):
            mixed = None
            for i in range(len(lses)):
                term = to_column(share[i, pl.ds(r, 1), :], queries) * read(i, r).astype(F32)
                mixed = term if mixed is None else mixed + term
            write(r, mixed)
            return carry

        lax.fori_loop(0, rows, one_row, 0)
        return peak + jnp.log2(total)

    for k in order:
        own = lax.rem(a + k, outer) * inner + b
        for j in range(1, inner):
            for copy in side_copies(k, j):
                copy.wait_recv()

        def read(i, r, k=k, own=own):
            return o_ref[own, r] if i == 0 else side_o[k, i, r]

        def write(r, mixed, k=k):
            pass_o[k, r] = mixed.astype(BF16)

        lses = [lse_ref[own]] + [side_l[k, j] for j in range(1, inner)]
        pass_l[k] = blend(lses, read, write)
        if k:
            for copy in line_copies(k):
                copy.start()
                sent.append(copy)
    for k in range(1, outer):
        for copy in line_copies(k):
            copy.wait_recv()

    def read(i, r):
        if i == outer:
            return s_ref[r]
        return pass_o[0, r] if i == 0 else line_o[i, r]

    group = queries // (kv * steps)

    def write(r, mixed):
        for c in range(kv):
            for t in range(steps):
                first = pl.multiple_of((r * steps + t) * (kv * group) + c * group, group)
                at = (c * steps + t) * group
                flat[pl.ds(first, group), :] = mixed[at:at + group]

    blend([pass_l[0]] + [line_l[k] for k in range(1, outer)] + [s_lse[...]], read, write)
    heads = kv * group
    for h in range(heads):
        att_all[me, :, h * width:(h + 1) * width] = flat[pl.ds(h, rows * steps, stride=heads), :].astype(BF16)
    gather = Gather(n, me, [att_all], gs1, gr1, gs2, gr2)
    gather.start()
    for k in range(1, outer):
        gather.forward(k)
    load.wait()
    gather.finish()

    columns = part.shape[2]
    tile = 256
    total_rows = n * rows * steps

    def project(i, carry):
        cols = pl.ds(pl.multiple_of(i * tile, tile), tile)
        lhs = att_all[...].reshape(total_rows, att_all.shape[2])
        done = jnp.dot(lhs, w_buf[:, cols], preferred_element_type=F32) + e_ref[:, cols].astype(F32)
        part[:, :, cols] = done.astype(BF16).reshape(heads_n, total_rows // heads_n, tile)
        return carry

    lax.fori_loop(0, columns // tile, project, 0)

    def head_copy(i):
        peer = lax.rem(head + i, heads_n)
        return remote(part.at[peer], landed.at[i], hs.at[i], hr.at[i], head=peer)

    for i in range(1, heads_n):
        copy = head_copy(i)
        copy.start()
        sent.append(copy)
    for i in range(1, heads_n):
        head_copy(i).wait_recv()
    total = part[head].astype(F32)
    for i in range(1, heads_n):
        total = total + landed[i].astype(F32)
    out_ref[...] = total.astype(BF16)
    for copy in sent:
        copy.wait_send()


def vmem():
    return pl.BlockSpec(memory_space=pltpu.VMEM)


def shards(n, heads_n, queries, new_kv, prompt_keys, prompt_values, suffix_kv, prompt_ids, suffix_lengths,
           token_ids, embedding, out_weight):
    steps, rows, heads, width = queries.shape
    prompts, positions, kv, _ = prompt_keys.shape
    group = heads // kv
    per = steps * group
    suf = suffix_kv.shape[2]
    all_rows = n * rows
    outer, inner = split_axis(n)
    scale2 = width ** -0.5 * math.log2(math.e)
    sds = jax.ShapeDtypeStruct
    dma = pltpu.SemaphoreType.DMA

    q_own = queries.reshape(steps, rows, kv, group, width).transpose(1, 2, 0, 3, 4).reshape(rows, kv, per, width)
    ids_own = jnp.broadcast_to(prompt_ids, (rows, 128))
    fresh = jnp.pad(new_kv.transpose(0, 2, 3, 1, 4), ((0, 0), (0, 0), (0, 0), (0, 16 - steps), (0, 0)))
    live = suf + 128
    q_all, ids_all, s_mixed, s_lse = pl.pallas_call(
        functools.partial(share_kernel, n, scale2, steps),
        out_shape=(sds((n, rows, kv, per, width), BF16), sds((n, rows, 128), jnp.int32),
                   sds((rows, kv * per, width), F32), sds((rows, 128), F32)),
        in_specs=[pl.BlockSpec(memory_space=pltpu.SMEM), vmem(), vmem(), vmem(), pl.BlockSpec(memory_space=pl.ANY)],
        out_specs=(vmem(),) * 4,
        scratch_shapes=[
            pltpu.VMEM((2, rows, suf * kv, width), BF16), pltpu.VMEM((2, suf * kv, width), F32),
            pltpu.VMEM((kv, live, width), BF16), pltpu.VMEM((kv, live, width), BF16), dma((1,)),
            *gather_sems(n, 2)],
        compiler_params=pltpu.CompilerParams(collective_id=0, has_side_effects=True, vmem_limit_bytes=VMEM_BYTES),
        name="share_queries",
    )(suffix_lengths.astype(jnp.int32), q_own, ids_own, fresh, suffix_kv.reshape(2, rows, suf * kv, width))

    tokens = all_rows * steps
    vocab = embedding.shape[0]
    local_ids = token_ids.reshape(tokens) - lax.axis_index("head") * vocab
    inside = (local_ids >= 0) & (local_ids < vocab)
    rem = jnp.broadcast_to(jnp.where(inside, local_ids % 16, -1)[:, None], (tokens, 128))
    tile = 4
    fixed = lambda *shape: pl.BlockSpec(shape, lambda p, *_: (0,) * len(shape))
    cut = pl.BlockSpec((1, positions * kv, width), lambda p, *_: (p, 0, 0))
    o_all, lse_all, embedded = pl.pallas_call(
        functools.partial(prompt_kernel, scale2, tile),
        out_shape=(sds((all_rows, kv * per, width), BF16), sds((all_rows, 128), F32), sds((tokens, embedding.shape[1]), BF16)),
        grid_spec=pltpu.PrefetchScalarGridSpec(
            num_scalar_prefetch=2, grid=(prompts,),
            in_specs=[fixed(all_rows, kv, per, width), cut, cut, fixed(tokens, 128), pl.BlockSpec(memory_space=pl.ANY)],
            out_specs=(fixed(all_rows, kv * per, width), fixed(all_rows, 128), fixed(tokens, embedding.shape[1])),
            scratch_shapes=[
                pltpu.SMEM((all_rows + tile,), jnp.int32), pltpu.VMEM((2, positions * kv, width), F32),
                pltpu.VMEM((kv, positions, width), BF16), pltpu.VMEM((kv, positions, width), BF16),
                pltpu.VMEM((tokens * 16, embedding.shape[1]), BF16), dma((1,))]),
        compiler_params=pltpu.CompilerParams(vmem_limit_bytes=VMEM_BYTES),
        name="prompt_attention",
    )(ids_all[:, :, 0].reshape(all_rows), local_ids, q_all.reshape(all_rows, kv, per, width),
      prompt_keys.reshape(prompts, positions * kv, width), prompt_values.reshape(prompts, positions * kv, width), rem, embedding)

    columns = out_weight.shape[1]
    out_rows = tokens // heads_n
    pair = dma((outer, inner))
    out = pl.pallas_call(
        functools.partial(finish_kernel, n, heads_n, steps, kv),
        out_shape=sds((out_rows, columns), BF16),
        in_specs=[vmem()] * 5 + [pl.BlockSpec(memory_space=pl.ANY)],
        out_specs=vmem(),
        scratch_shapes=[
            pltpu.VMEM((outer, inner, rows, kv * per, width), BF16), pltpu.VMEM((outer, inner, rows, 128), F32),
            pltpu.VMEM((outer, rows, kv * per, width), BF16), pltpu.VMEM((outer, rows, 128), F32),
            pltpu.VMEM((outer, rows, kv * per, width), BF16), pltpu.VMEM((outer, rows, 128), F32),
            pltpu.VMEM((max(inner, outer + 1), rows, 128), F32), pltpu.VMEM((rows * kv * per, width), F32),
            pltpu.VMEM((n, rows * steps, heads * width), BF16), pltpu.VMEM(out_weight.shape, BF16),
            pltpu.VMEM((heads_n, out_rows, columns), BF16), pltpu.VMEM((heads_n, out_rows, columns), BF16),
            dma((1,)), pair, pair, pair, pair, dma((outer,)), dma((outer,)), dma((outer,)), dma((outer,)),
            *gather_sems(n, 1), dma((heads_n,)), dma((heads_n,))],
        compiler_params=pltpu.CompilerParams(collective_id=1, has_side_effects=True, vmem_limit_bytes=VMEM_BYTES),
        name="finish",
    )(o_all.reshape(n, rows, kv * per, width), lse_all.reshape(n, rows, 128), s_mixed, s_lse, embedded, out_weight)
    return out.reshape(all_rows // heads_n, steps, columns)


def solution(mesh):
    return jax.shard_map(
        functools.partial(shards, mesh.shape["seq"], mesh.shape["head"]),
        mesh=mesh,
        in_specs=(
            P(None, "seq", "head", None),
            P(None, None, "seq", "head", None),
            P(None, "seq", "head", None),
            P(None, "seq", "head", None),
            P(None, "seq", None, "head", None),
            P("seq", None),
            P("seq"),
            P(),
            P("head", "seq"),
            P("head", "seq"),
        ),
        out_specs=P("head", None, "seq"),
        check_vma=False,
    )
```

```python
import functools
import math

import jax
import jax.numpy as jnp
from jax import lax
from jax.experimental import pallas as pl
from jax.experimental.pallas import tpu as pltpu
from jax.sharding import PartitionSpec as P

MESH = pl.DeviceIdType.MESH
F32 = jnp.float32
BF16 = jnp.bfloat16
NT = (((1,), (1,)), ((), ()))
VMEM_BYTES = 58 * 2**20


def split_axis(n):
    inner = 2 if n <= 8 else 8
    return n // inner, inner


def greet(peers):
    barrier = pltpu.get_barrier_semaphore()
    for peer in peers:
        pl.semaphore_signal(barrier, inc=1, device_id=peer, device_id_type=MESH)
    pl.semaphore_wait(barrier, len(peers))


def seq_peers(n, me):
    outer, inner = split_axis(n)
    a, b = me // inner, lax.rem(me, inner)
    line = [lax.rem(a + k, outer) * inner + b for k in range(outer)]
    side = [a * inner + lax.rem(b + j, inner) for j in range(inner)]
    return line, side


class Gather:
    def __init__(self, n, me, bufs, send1, recv1, send2, recv2):
        self.n, self.me, self.bufs = n, me, bufs
        self.outer, self.inner = split_axis(n)
        self.sems = (send1, recv1, send2, recv2)
        self.a, self.b = me // self.inner, lax.rem(me, self.inner)
        self.sent = []

    def shard(self, k, j):
        a = lax.rem(self.a - k + self.outer, self.outer)
        b = lax.rem(self.b - j + self.inner, self.inner)
        return a * self.inner + b

    def copy1(self, i, k, shard):
        send1, recv1, _, _ = self.sems
        peer = lax.rem(self.a + k, self.outer) * self.inner + self.b
        buf = self.bufs[i]
        return pltpu.make_async_remote_copy(
            src_ref=buf.at[shard], dst_ref=buf.at[shard], send_sem=send1.at[i, k], recv_sem=recv1.at[i, k],
            device_id={"seq": peer}, device_id_type=MESH)

    def copy2(self, i, k, j, shard):
        _, _, send2, recv2 = self.sems
        peer = self.a * self.inner + lax.rem(self.b + j, self.inner)
        buf = self.bufs[i]
        return pltpu.make_async_remote_copy(
            src_ref=buf.at[shard], dst_ref=buf.at[shard], send_sem=send2.at[i, k, j], recv_sem=recv2.at[i, k, j],
            device_id={"seq": peer}, device_id_type=MESH)

    def begin(self, copy):
        copy.start()
        self.sent.append(copy)

    def start(self):
        for k in range(1, self.outer):
            for i in range(len(self.bufs)):
                self.begin(self.copy1(i, k, self.me))
        self.forward(0)

    def forward(self, k):
        shard = self.shard(k, 0)
        for i in range(len(self.bufs)):
            if k:
                self.copy1(i, k, shard).wait_recv()
            for j in range(1, self.inner):
                self.begin(self.copy2(i, k, j, shard))

    def finish(self):
        for k in range(self.outer):
            for j in range(1, self.inner):
                for i in range(len(self.bufs)):
                    self.copy2(i, k, j, self.shard(k, j)).wait_recv()
        for copy in self.sent:
            copy.wait_send()


def gather_sems(n, count):
    outer, inner = split_axis(n)
    line = pltpu.SemaphoreType.DMA((count, outer))
    side = pltpu.SemaphoreType.DMA((count, outer, inner))
    return [line, line, side, side]


def eye(rows, lanes=128):
    return lax.broadcasted_iota(jnp.int32, (rows, lanes), 0) == lax.broadcasted_iota(jnp.int32, (rows, lanes), 1)


def to_row(column):
    return jnp.sum(jnp.where(eye(column.shape[0]), column, 0.0), axis=0, keepdims=True)


def to_column(row, rows):
    return jnp.sum(jnp.where(eye(rows), row, 0.0), axis=1, keepdims=True)


def weigh(scores, scale2):
    peak = jnp.max(scores, axis=-1, keepdims=True)
    weights = jnp.exp2((scores - peak) * scale2)
    total = jnp.sum(weights, axis=-1, keepdims=True)
    return weights.astype(BF16), 1.0 / total, peak * scale2 + jnp.log2(total)


def share_kernel(n, scale2, steps, lengths, prompt_ids, q_own, fresh, suffix, q_all, ids_all, mixed_ref, lse_ref,
                 raw, wide, keys, values, local_sem, send1, recv1, send2, recv2):
    rows, kv, queries, width = q_own.shape
    suf = suffix.shape[2] // kv
    live = keys.shape[1]
    me = lax.axis_index("seq")
    line, side = seq_peers(n, me)
    greet([{"seq": d} for d in line[1:] + side[1:]])
    q_all[me] = q_own[...]
    sublane = lax.broadcasted_iota(jnp.int32, (rows, 128), 0)
    ids_own = jnp.zeros((rows, 128), jnp.int32)
    for r in range(rows):
        ids_own = jnp.where(sublane == r, prompt_ids[r, 0], ids_own)
    ids_all[me] = ids_own
    gather = Gather(n, me, [q_all, ids_all], send1, recv1, send2, recv2)
    gather.start()
    load = pltpu.make_async_copy(suffix, raw, local_sem.at[0])
    load.start()
    keys[...] = jnp.zeros_like(keys)
    values[...] = jnp.zeros_like(values)
    column = lax.broadcasted_iota(jnp.int32, (queries, live), 1)
    step = lax.broadcasted_iota(jnp.int32, (queries, live), 0) // (queries // steps)
    new = jnp.logical_and(column >= suf, column - suf <= step)
    load.wait()

    def one_row(r, carry):
        old = column < lengths[r]
        stats = []
        for part, store in ((0, keys), (1, values)):
            wide[part] = raw[part, r].astype(F32)
            for c in range(kv):
                store[c, 0:suf] = wide[part, pl.ds(c, suf, stride=kv), :].astype(BF16)
                store[c, suf:suf + fresh.shape[3]] = fresh[part, r, c]
        seen = jnp.logical_or(old, new)
        scores = [lax.dot_general(q_own[r, c], keys[c], NT, preferred_element_type=F32) for c in range(kv)]
        weighed = [weigh(jnp.where(seen, x, -jnp.inf), scale2) for x in scores]
        for c, (weights, inverse, lse) in enumerate(weighed):
            mixed = jnp.dot(weights, values[c], preferred_element_type=F32)
            mixed_ref[r, c * queries:(c + 1) * queries] = mixed * inverse
            stats.append(lse)
        lse_ref[pl.ds(r, 1), :] = to_row(jnp.concatenate(stats, axis=0))
        return carry

    outer = gather.outer
    for k in range(outer):
        lax.fori_loop(rows * k // outer, rows * (k + 1) // outer, one_row, 0)
        if k + 1 < outer:
            gather.forward(k + 1)
    gather.finish()


def prompt_kernel(scale2, tile, tokens_ref, ids, q_ref, k_ref, v_ref, embedding, o_ref, lse_ref, blocks,
                  order, counts, wide, keys, values, sem):
    p = pl.program_id(0)
    prompts = counts.shape[0]
    rows, kv, queries, width = q_ref.shape
    positions = k_ref.shape[1] // kv
    vocab = embedding.shape[0]
    token_rows, steps = tokens_ref.shape
    tokens = token_rows * steps
    room = rows + tile

    @pl.when(p == 0)
    def _():
        first_id = lax.axis_index("head") * vocab

        def fetch(r, carry):
            for t in range(steps):
                local = jnp.clip(tokens_ref[r, t] - first_id, 0, vocab - 1)
                first = pl.multiple_of(local // 16 * 16, 16)
                to = pl.multiple_of((r * steps + t) * 16, 16)
                pltpu.make_async_copy(embedding.at[pl.ds(first, 16)], blocks.at[pl.ds(to, 16)], sem.at[0]).start()
            return carry

        for i in range(prompts):
            counts[i] = 0

        def place(r, carry):
            mine = ids[r, 0]
            count = counts[mine]
            order[mine * room + count] = r
            counts[mine] = count + 1
            return carry

        lax.fori_loop(0, token_rows, fetch, 0)
        lax.fori_loop(0, rows, place, 0)

    count = counts[p]
    base = p * room
    last = order[base + jnp.maximum(count - 1, 0)]
    for j in range(tile):
        order[base + count + j] = last
    for source, store, part in ((k_ref, keys, 0), (v_ref, values, 1)):
        wide[part] = source[0].astype(F32)
        for c in range(kv):
            store[c] = wide[part, pl.ds(c, positions, stride=kv), :].astype(BF16)

    def one_tile(i, carry):
        picked = [order[base + i * tile + j] for j in range(tile)]
        scores = []
        for c in range(kv):
            query = jnp.concatenate([q_ref[r, c] for r in picked], axis=0)
            scores.append(lax.dot_general(query, keys[c], NT, preferred_element_type=F32))
        weighed = [weigh(x, scale2) for x in scores]
        for c, (weights, inverse, _) in enumerate(weighed):
            mixed = (jnp.dot(weights, values[c], preferred_element_type=F32) * inverse).astype(BF16)
            for j, r in enumerate(picked):
                o_ref[r, c * queries:(c + 1) * queries] = mixed[j * queries:(j + 1) * queries]
        for j, r in enumerate(picked):
            span = slice(j * queries, (j + 1) * queries)
            lse_ref[pl.ds(r, 1), :] = to_row(jnp.concatenate([w[2][span] for w in weighed], axis=0))
        return carry

    lax.fori_loop(0, (count + tile - 1) // tile, one_tile, 0)

    @pl.when(p == pl.num_programs(0) - 1)
    def _():
        span = min(vocab, tokens * 16)
        for i in range(tokens * 16 // span):
            pltpu.make_async_copy(embedding.at[pl.ds(0, span)], blocks.at[pl.ds(i * span, span)], sem.at[0]).wait()


def finish_kernel(n, heads_n, steps, kv, vocab_own, o_ref, lse_ref, s_ref, s_lse, tokens_ref, weight, blocks, out_ref,
                  side_o, side_l, line_o, line_l, pass_o, pass_l, share, flat, att_all, w_buf, e_buf, block_buf, part, landed,
                  local_sem, so1, ro1, sl1, rl1, so2, ro2, sl2, rl2, gs1, gr1, gs2, gr2, hs, hr):
    rows, queries, width = s_ref.shape
    outer, inner = split_axis(n)
    me = lax.axis_index("seq")
    head = lax.axis_index("head")
    line, side = seq_peers(n, me)
    a, b = me // inner, lax.rem(me, inner)
    load = pltpu.make_async_copy(weight, w_buf, local_sem.at[0])
    load.start()
    fetch = pltpu.make_async_copy(blocks, block_buf, local_sem.at[1])
    fetch.start()
    greet([{"seq": d} for d in line[1:] + side[1:]] + [{"head": lax.rem(head + i, heads_n)} for i in range(1, heads_n)])
    order = list(range(1, outer)) + [0]

    def remote(src, dst, send, recv, **to):
        return pltpu.make_async_remote_copy(src_ref=src, dst_ref=dst, send_sem=send, recv_sem=recv, device_id=to, device_id_type=MESH)

    def side_copies(k, j):
        shard = lax.rem(a + k, outer) * inner + lax.rem(b + j, inner)
        return [remote(o_ref.at[shard], side_o.at[k, j], so1.at[k, j], ro1.at[k, j], seq=side[j]),
                remote(lse_ref.at[shard], side_l.at[k, j], sl1.at[k, j], rl1.at[k, j], seq=side[j])]

    def line_copies(k):
        return [remote(pass_o.at[k], line_o.at[k], so2.at[k], ro2.at[k], seq=line[k]),
                remote(pass_l.at[k], line_l.at[k], sl2.at[k], rl2.at[k], seq=line[k])]

    sent = []
    for k in order:
        for j in range(1, inner):
            for copy in side_copies(k, j):
                copy.start()
                sent.append(copy)

    def blend(lses, read, write):
        peak = functools.reduce(jnp.maximum, lses)
        raw = [jnp.exp2(l - peak) for l in lses]
        total = functools.reduce(jnp.add, raw)
        for i, w in enumerate(raw):
            share[i] = w / total

        def one_row(r, carry):
            mixed = None
            for i in range(len(lses)):
                term = to_column(share[i, pl.ds(r, 1), :], queries) * read(i, r).astype(F32)
                mixed = term if mixed is None else mixed + term
            write(r, mixed)
            return carry

        lax.fori_loop(0, rows, one_row, 0, unroll=4)
        return peak + jnp.log2(total)

    for k in order:
        own = lax.rem(a + k, outer) * inner + b
        for j in range(1, inner):
            for copy in side_copies(k, j):
                copy.wait_recv()

        def read(i, r, k=k, own=own):
            return o_ref[own, r] if i == 0 else side_o[k, i, r]

        def write(r, mixed, k=k):
            pass_o[k, r] = mixed.astype(BF16)

        lses = [lse_ref[own]] + [side_l[k, j] for j in range(1, inner)]
        pass_l[k] = blend(lses, read, write)
        if k:
            for copy in line_copies(k):
                copy.start()
                sent.append(copy)
    for k in range(1, outer):
        for copy in line_copies(k):
            copy.wait_recv()

    def read(i, r):
        if i == outer:
            return s_ref[r]
        return pass_o[0, r] if i == 0 else line_o[i, r]

    group = queries // (kv * steps)

    def write(r, mixed):
        for c in range(kv):
            for t in range(steps):
                first = pl.multiple_of((r * steps + t) * (kv * group) + c * group, group)
                at = (c * steps + t) * group
                flat[pl.ds(first, group), :] = mixed[at:at + group]

    blend([pass_l[0]] + [line_l[k] for k in range(1, outer)] + [s_lse[...]], read, write)
    heads = kv * group
    for h in range(heads):
        att_all[me, :, h * width:(h + 1) * width] = flat[pl.ds(h, rows * steps, stride=heads), :].astype(BF16)
    gather = Gather(n, me, [att_all], gs1, gr1, gs2, gr2)
    gather.start()

    vocab, (token_rows, _) = vocab_own, tokens_ref.shape
    first_id = head * vocab
    each = 16 // steps
    lane = lax.broadcasted_iota(jnp.int32, (16, 256), 1)
    owner = lane // 16 == lax.broadcasted_iota(jnp.int32, (16, 256), 0)
    fetch.wait()

    def pick(i, carry):
        wanted = jnp.full((16, 256), -1, jnp.int32)
        for x in range(16):
            token = tokens_ref[i * each + x // steps, x % steps] - first_id
            inside = jnp.logical_and(token >= 0, token < vocab)
            wanted = jnp.where(lane // 16 == x, jnp.where(inside, lax.rem(token, 16), -1), wanted)
        chosen = jnp.logical_and(owner, lax.rem(lane, 16) == wanted).astype(F32).astype(BF16)
        block = block_buf[pl.ds(pl.multiple_of(i * 256, 256), 256), :]
        e_buf[pl.ds(pl.multiple_of(i * 16, 16), 16), :] = jnp.dot(chosen, block, preferred_element_type=F32)
        return carry

    groups = token_rows * steps // 16
    for k in range(1, outer):
        lax.fori_loop(groups * (k - 1) // outer, groups * k // outer, pick, 0)
        gather.forward(k)
    lax.fori_loop(groups * (outer - 1) // outer, groups, pick, 0)
    load.wait()

    columns = part.shape[2]
    tile = min(256, columns)
    chunk = rows * steps
    span = n // heads_n

    def project(j, cols):
        where = lax.rem(b + j, inner)
        lhs = jnp.concatenate([att_all[x * inner + where] for x in range(outer)], axis=0)
        done = jnp.dot(lhs, w_buf[:, cols], preferred_element_type=F32)
        for x in range(outer):
            shard = x * inner + where
            at = pl.ds(pl.multiple_of(shard * chunk, chunk), chunk)
            part[shard, :, cols] = (done[x * chunk:(x + 1) * chunk] + e_buf[at, cols]).astype(BF16)

    def head_copy(i, q, cols):
        peer = lax.rem(head + i, heads_n)
        return remote(part.at[pl.ds(peer * span, span), :, cols], landed.at[i, :, :, cols], hs.at[i, q], hr.at[i, q], head=peer)

    cuts = [slice(x, x + tile) for x in range(0, columns, tile)]
    for cols in cuts:
        project(0, cols)
    gather.finish()
    for q, cols in enumerate(cuts):
        for j in range(1, inner):
            project(j, cols)
        for i in range(1, heads_n):
            copy = head_copy(i, q, cols)
            copy.start()
            sent.append(copy)
    for q, cols in enumerate(cuts):
        for i in range(1, heads_n):
            head_copy(i, q, cols).wait_recv()
        total = part[pl.ds(head * span, span), :, cols].astype(F32)
        for i in range(1, heads_n):
            total = total + landed[i, :, :, cols].astype(F32)
        out_ref[:, cols] = total.astype(BF16).reshape(span * chunk, tile)
    for copy in sent:
        copy.wait_send()


def smem():
    return pl.BlockSpec(memory_space=pltpu.SMEM)


def vmem():
    return pl.BlockSpec(memory_space=pltpu.VMEM)


def shards(n, heads_n, queries, new_kv, prompt_keys, prompt_values, suffix_kv, prompt_ids, suffix_lengths,
           token_ids, embedding, out_weight):
    steps, rows, heads, width = queries.shape
    prompts, positions, kv, _ = prompt_keys.shape
    group = heads // kv
    per = steps * group
    suf = suffix_kv.shape[2]
    all_rows = n * rows
    outer, inner = split_axis(n)
    scale2 = width ** -0.5 * math.log2(math.e)
    sds = jax.ShapeDtypeStruct
    dma = pltpu.SemaphoreType.DMA

    q_own = queries.reshape(steps, rows, kv, group, width).transpose(1, 2, 0, 3, 4).reshape(rows, kv, per, width)
    fresh = jnp.pad(new_kv.transpose(0, 2, 3, 1, 4), ((0, 0), (0, 0), (0, 0), (0, 16 - steps), (0, 0)))
    live = suf + 128
    q_all, ids_all, s_mixed, s_lse = pl.pallas_call(
        functools.partial(share_kernel, n, scale2, steps),
        out_shape=(sds((n, rows, kv, per, width), BF16), sds((n, rows, 128), jnp.int32),
                   sds((rows, kv * per, width), F32), sds((rows, 128), F32)),
        in_specs=[smem(), smem(), vmem(), vmem(), pl.BlockSpec(memory_space=pl.ANY)],
        out_specs=(vmem(),) * 4,
        scratch_shapes=[
            pltpu.VMEM((2, rows, suf * kv, width), BF16), pltpu.VMEM((2, suf * kv, width), F32),
            pltpu.VMEM((kv, live, width), BF16), pltpu.VMEM((kv, live, width), BF16), dma((1,)),
            *gather_sems(n, 2)],
        compiler_params=pltpu.CompilerParams(collective_id=0, has_side_effects=True, vmem_limit_bytes=VMEM_BYTES),
        name="share_queries",
    )(suffix_lengths.astype(jnp.int32), prompt_ids.astype(jnp.int32), q_own, fresh, suffix_kv.reshape(2, rows, suf * kv, width))

    tokens = all_rows * steps
    vocab = embedding.shape[0]
    tile = 4
    fixed = lambda *shape: pl.BlockSpec(shape, lambda p, *_: (0,) * len(shape))
    cut = pl.BlockSpec((1, positions * kv, width), lambda p, *_: (p, 0, 0))
    o_all, lse_all, blocks = pl.pallas_call(
        functools.partial(prompt_kernel, scale2, tile),
        out_shape=(sds((all_rows, kv * per, width), BF16), sds((all_rows, 128), F32), sds((tokens * 16, embedding.shape[1]), BF16)),
        grid=(prompts,),
        in_specs=[smem(), smem(), fixed(all_rows, kv, per, width), cut, cut, pl.BlockSpec(memory_space=pl.ANY)],
        out_specs=(fixed(all_rows, kv * per, width), fixed(all_rows, 128), pl.BlockSpec(memory_space=pl.ANY)),
        scratch_shapes=[
            pltpu.SMEM((prompts * (all_rows + tile),), jnp.int32), pltpu.SMEM((prompts,), jnp.int32),
            pltpu.VMEM((2, positions * kv, width), F32),
            pltpu.VMEM((kv, positions, width), BF16), pltpu.VMEM((kv, positions, width), BF16), dma((1,))],
        compiler_params=pltpu.CompilerParams(vmem_limit_bytes=VMEM_BYTES),
        name="prompt_attention",
    )(token_ids, ids_all.reshape(all_rows, 128), q_all.reshape(all_rows, kv, per, width),
      prompt_keys.reshape(prompts, positions * kv, width), prompt_values.reshape(prompts, positions * kv, width), embedding)

    columns = out_weight.shape[1]
    out_rows = tokens // heads_n
    pair = dma((outer, inner))
    out = pl.pallas_call(
        functools.partial(finish_kernel, n, heads_n, steps, kv, embedding.shape[0]),
        out_shape=sds((out_rows, columns), BF16),
        in_specs=[vmem()] * 4 + [smem()] + [pl.BlockSpec(memory_space=pl.ANY)] * 2,
        out_specs=vmem(),
        scratch_shapes=[
            pltpu.VMEM((outer, inner, rows, kv * per, width), BF16), pltpu.VMEM((outer, inner, rows, 128), F32),
            pltpu.VMEM((outer, rows, kv * per, width), BF16), pltpu.VMEM((outer, rows, 128), F32),
            pltpu.VMEM((outer, rows, kv * per, width), BF16), pltpu.VMEM((outer, rows, 128), F32),
            pltpu.VMEM((max(inner, outer + 1), rows, 128), F32), pltpu.VMEM((rows * kv * per, width), F32),
            pltpu.VMEM((n, rows * steps, heads * width), BF16), pltpu.VMEM(out_weight.shape, BF16),
            pltpu.VMEM((tokens, columns), F32), pltpu.VMEM(blocks.shape, BF16),
            pltpu.VMEM((n, rows * steps, columns), BF16), pltpu.VMEM((heads_n, n // heads_n, rows * steps, columns), BF16),
            dma((2,)), pair, pair, pair, pair, dma((outer,)), dma((outer,)), dma((outer,)), dma((outer,)),
            *gather_sems(n, 1), dma((heads_n, 8)), dma((heads_n, 8))],
        compiler_params=pltpu.CompilerParams(collective_id=1, has_side_effects=True, vmem_limit_bytes=VMEM_BYTES),
        name="finish",
    )(o_all.reshape(n, rows, kv * per, width), lse_all.reshape(n, rows, 128), s_mixed, s_lse, token_ids, out_weight, blocks)
    return out.reshape(all_rows // heads_n, steps, columns)


def solution(mesh):
    return jax.shard_map(
        functools.partial(shards, mesh.shape["seq"], mesh.shape["head"]),
        mesh=mesh,
        in_specs=(
            P(None, "seq", "head", None),
            P(None, None, "seq", "head", None),
            P(None, "seq", "head", None),
            P(None, "seq", "head", None),
            P(None, "seq", None, "head", None),
            P("seq", None),
            P("seq"),
            P(),
            P("head", "seq"),
            P("head", "seq"),
        ),
        out_specs=P("head", None, "seq"),
        check_vma=False,
    )
```

```python
import functools
import math

import jax
import jax.numpy as jnp
from jax import lax
from jax.experimental import pallas as pl
from jax.experimental.pallas import tpu as pltpu
from jax.sharding import PartitionSpec as P

MESH = pl.DeviceIdType.MESH
F32 = jnp.float32
BF16 = jnp.bfloat16
NT = (((1,), (1,)), ((), ()))
VMEM_BYTES = 58 * 2**20


def split_axis(n):
    inner = 2 if n <= 8 else 8
    return n // inner, inner


def greet(peers):
    barrier = pltpu.get_barrier_semaphore()
    for peer in peers:
        pl.semaphore_signal(barrier, inc=1, device_id=peer, device_id_type=MESH)
    pl.semaphore_wait(barrier, len(peers))


def seq_peers(n, me):
    outer, inner = split_axis(n)
    a, b = me // inner, lax.rem(me, inner)
    line = [lax.rem(a + k, outer) * inner + b for k in range(outer)]
    side = [a * inner + lax.rem(b + j, inner) for j in range(inner)]
    return line, side


class Gather:
    def __init__(self, n, me, bufs, send1, recv1, send2, recv2):
        self.n, self.me, self.bufs = n, me, bufs
        self.outer, self.inner = split_axis(n)
        self.sems = (send1, recv1, send2, recv2)
        self.a, self.b = me // self.inner, lax.rem(me, self.inner)
        self.sent = []

    def shard(self, k, j):
        a = lax.rem(self.a - k + self.outer, self.outer)
        b = lax.rem(self.b - j + self.inner, self.inner)
        return a * self.inner + b

    def copy1(self, i, k, shard):
        send1, recv1, _, _ = self.sems
        peer = lax.rem(self.a + k, self.outer) * self.inner + self.b
        buf = self.bufs[i]
        return pltpu.make_async_remote_copy(
            src_ref=buf.at[shard], dst_ref=buf.at[shard], send_sem=send1.at[i, k], recv_sem=recv1.at[i, k],
            device_id={"seq": peer}, device_id_type=MESH)

    def copy2(self, i, k, j, shard):
        _, _, send2, recv2 = self.sems
        peer = self.a * self.inner + lax.rem(self.b + j, self.inner)
        buf = self.bufs[i]
        return pltpu.make_async_remote_copy(
            src_ref=buf.at[shard], dst_ref=buf.at[shard], send_sem=send2.at[i, k, j], recv_sem=recv2.at[i, k, j],
            device_id={"seq": peer}, device_id_type=MESH)

    def begin(self, copy):
        copy.start()
        self.sent.append(copy)

    def start(self):
        for k in range(1, self.outer):
            for i in range(len(self.bufs)):
                self.begin(self.copy1(i, k, self.me))
        self.forward(0)

    def forward(self, k):
        shard = self.shard(k, 0)
        for i in range(len(self.bufs)):
            if k:
                self.copy1(i, k, shard).wait_recv()
            for j in range(1, self.inner):
                self.begin(self.copy2(i, k, j, shard))

    def finish(self):
        for k in range(self.outer):
            for j in range(1, self.inner):
                for i in range(len(self.bufs)):
                    self.copy2(i, k, j, self.shard(k, j)).wait_recv()
        for copy in self.sent:
            copy.wait_send()


def gather_sems(n, count):
    outer, inner = split_axis(n)
    line = pltpu.SemaphoreType.DMA((count, outer))
    side = pltpu.SemaphoreType.DMA((count, outer, inner))
    return [line, line, side, side]


def eye(rows, lanes=128):
    return lax.broadcasted_iota(jnp.int32, (rows, lanes), 0) == lax.broadcasted_iota(jnp.int32, (rows, lanes), 1)


def to_row(column):
    return jnp.sum(jnp.where(eye(column.shape[0]), column, 0.0), axis=0, keepdims=True)


def to_column(row, rows):
    return jnp.sum(jnp.where(eye(rows), row, 0.0), axis=1, keepdims=True)


def weigh(scores, scale2):
    peak = jnp.max(scores, axis=-1, keepdims=True)
    weights = jnp.exp2((scores - peak) * scale2)
    total = jnp.sum(weights, axis=-1, keepdims=True)
    return weights.astype(BF16), 1.0 / total, peak * scale2 + jnp.log2(total)


def share_kernel(n, scale2, steps, lengths, prompt_ids, q_own, fresh, suffix, q_all, ids_all, mixed_ref, lse_ref,
                 raw, wide, keys, values, local_sem, send1, recv1, send2, recv2):
    rows, kv, queries, width = q_own.shape
    suf = suffix.shape[2] // kv
    live = keys.shape[1]
    me = lax.axis_index("seq")
    line, side = seq_peers(n, me)
    greet([{"seq": d} for d in line[1:] + side[1:]])
    q_all[me] = q_own[...]
    sublane = lax.broadcasted_iota(jnp.int32, (rows, 128), 0)
    ids_own = jnp.zeros((rows, 128), jnp.int32)
    for r in range(rows):
        ids_own = jnp.where(sublane == r, prompt_ids[0, r], ids_own)
    ids_all[me] = ids_own
    gather = Gather(n, me, [q_all, ids_all], send1, recv1, send2, recv2)
    gather.start()
    load = pltpu.make_async_copy(suffix, raw, local_sem.at[0])
    load.start()
    keys[...] = jnp.zeros_like(keys)
    values[...] = jnp.zeros_like(values)
    column = lax.broadcasted_iota(jnp.int32, (queries, live), 1)
    step = lax.broadcasted_iota(jnp.int32, (queries, live), 0) // (queries // steps)
    new = jnp.logical_and(column >= suf, column - suf <= step)
    load.wait()

    def one_row(r, carry):
        old = column < lengths[r]
        stats = []
        for part, store in ((0, keys), (1, values)):
            wide[part] = raw[part, r].astype(F32)
            late = [fresh[part, u, r].astype(F32) for u in range(steps)]
            for c in range(kv):
                store[c, 0:suf] = wide[part, pl.ds(c, suf, stride=kv), :].astype(BF16)
                rows16 = [x[c:c + 1] for x in late] + [jnp.zeros((16 - steps, width), F32)]
                store[c, suf:suf + 16] = jnp.concatenate(rows16, axis=0).astype(BF16)
        seen = jnp.logical_or(old, new)
        scores = [lax.dot_general(q_own[r, c], keys[c], NT, preferred_element_type=F32) for c in range(kv)]
        weighed = [weigh(jnp.where(seen, x, -jnp.inf), scale2) for x in scores]
        for c, (weights, inverse, lse) in enumerate(weighed):
            mixed = jnp.dot(weights, values[c], preferred_element_type=F32)
            mixed_ref[r, c * queries:(c + 1) * queries] = mixed * inverse
            stats.append(lse)
        lse_ref[pl.ds(r, 1), :] = to_row(jnp.concatenate(stats, axis=0))
        return carry

    outer = gather.outer
    for k in range(outer):
        lax.fori_loop(rows * k // outer, rows * (k + 1) // outer, one_row, 0)
        if k + 1 < outer:
            gather.forward(k + 1)
    gather.finish()


def prompt_kernel(scale2, tile, tokens_ref, ids, q_ref, k_ref, v_ref, embedding, o_ref, lse_ref, blocks,
                  order, counts, wide, keys, values, staged, sem):
    p = pl.program_id(0)
    prompts = counts.shape[0]
    rows, kv, queries, width = q_ref.shape
    positions = k_ref.shape[1] // kv
    vocab = embedding.shape[0]
    steps, token_rows = tokens_ref.shape
    tokens = token_rows * steps
    room = rows + tile

    @pl.when(p == 0)
    def _():
        def fetch(r, carry):
            for t in range(steps):
                local = lax.rem(tokens_ref[t, r], vocab)
                first = pl.multiple_of(local // 16 * 16, 16)
                to = pl.multiple_of((r * steps + t) * 16, 16)
                pltpu.make_async_copy(embedding.at[pl.ds(first, 16)], staged.at[pl.ds(to, 16)], sem.at[0]).start()
            return carry

        for i in range(prompts):
            counts[i] = 0
        values[:, :, width:] = jnp.ones((kv, positions, width), BF16)

        def place(r, carry):
            mine = ids[r, 0]
            count = counts[mine]
            order[mine * room + count] = r
            counts[mine] = count + 1
            return carry

        lax.fori_loop(0, token_rows, fetch, 0)
        lax.fori_loop(0, rows, place, 0)

    count = counts[p]
    base = p * room
    last = order[base + jnp.maximum(count - 1, 0)]
    for j in range(tile):
        order[base + count + j] = last
    for source, store, part in ((k_ref, keys, 0), (v_ref, values, 1)):
        wide[part] = source[0].astype(F32)
        for c in range(kv):
            store[c, :, 0:width] = wide[part, pl.ds(c, positions, stride=kv), :].astype(BF16)

    def one_tile(i, carry):
        picked = [order[base + i * tile + j] for j in range(tile)]
        scores = []
        for c in range(kv):
            query = jnp.concatenate([q_ref[r, c] for r in picked], axis=0)
            scores.append(lax.dot_general(query, keys[c], NT, preferred_element_type=F32))
        lses = []
        for c, score in enumerate(scores):
            peak = jnp.max(score, axis=-1, keepdims=True)
            weights = jnp.exp2((score - peak) * scale2).astype(BF16)
            both = jnp.dot(weights, values[c], preferred_element_type=F32)
            lses.append(peak * scale2 + jnp.log2(both[:, width:]))
            mixed = (both[:, :width] / both[:, width:]).astype(BF16)
            for j, r in enumerate(picked):
                o_ref[r, c * queries:(c + 1) * queries] = mixed[j * queries:(j + 1) * queries]
        for j, r in enumerate(picked):
            span = slice(j * queries, (j + 1) * queries)
            lse_ref[pl.ds(r, 1), :] = to_row(jnp.concatenate([x[span] for x in lses], axis=0))
        return carry

    lax.fori_loop(0, (count + tile - 1) // tile, one_tile, 0)

    @pl.when(p == pl.num_programs(0) // 2)
    def _():
        span = min(vocab, tokens * 16)
        for i in range(tokens * 16 // span):
            pltpu.make_async_copy(embedding.at[pl.ds(0, span)], staged.at[pl.ds(i * span, span)], sem.at[0]).wait()
        pltpu.make_async_copy(staged, blocks, sem.at[1]).start()

    @pl.when(p == pl.num_programs(0) - 1)
    def _():
        pltpu.make_async_copy(staged, blocks, sem.at[1]).wait()


def finish_kernel(n, heads_n, steps, kv, vocab_own, o_ref, lse_ref, s_ref, s_lse, tokens_ref, weight, blocks, out_ref,
                  side_o, side_l, line_o, line_l, pass_o, pass_l, share, flat, att_all, w_buf, e_buf, block_buf, part, landed,
                  local_sem, so1, ro1, sl1, rl1, so2, ro2, sl2, rl2, gs1, gr1, gs2, gr2, hs, hr):
    rows, queries, width = s_ref.shape
    outer, inner = split_axis(n)
    me = lax.axis_index("seq")
    head = lax.axis_index("head")
    line, side = seq_peers(n, me)
    a, b = me // inner, lax.rem(me, inner)
    load = pltpu.make_async_copy(weight, w_buf, local_sem.at[0])
    load.start()
    fetch = pltpu.make_async_copy(blocks, block_buf, local_sem.at[1])
    fetch.start()
    greet([{"seq": d} for d in line[1:] + side[1:]] + [{"head": lax.rem(head + i, heads_n)} for i in range(1, heads_n)])
    order = list(range(1, outer)) + [0]

    def remote(src, dst, send, recv, **to):
        return pltpu.make_async_remote_copy(src_ref=src, dst_ref=dst, send_sem=send, recv_sem=recv, device_id=to, device_id_type=MESH)

    def side_copies(k, j):
        shard = lax.rem(a + k, outer) * inner + lax.rem(b + j, inner)
        return [remote(o_ref.at[shard], side_o.at[k, j], so1.at[k, j], ro1.at[k, j], seq=side[j]),
                remote(lse_ref.at[shard], side_l.at[k, j], sl1.at[k, j], rl1.at[k, j], seq=side[j])]

    def line_copies(k):
        return [remote(pass_o.at[k], line_o.at[k], so2.at[k], ro2.at[k], seq=line[k]),
                remote(pass_l.at[k], line_l.at[k], sl2.at[k], rl2.at[k], seq=line[k])]

    sent = []
    for k in order:
        for j in range(1, inner):
            for copy in side_copies(k, j):
                copy.start()
                sent.append(copy)

    def blend(lses, read, write):
        peak = functools.reduce(jnp.maximum, lses)
        raw = [jnp.exp2(l - peak) for l in lses]
        total = functools.reduce(jnp.add, raw)
        for i, w in enumerate(raw):
            share[i] = w / total

        def one_row(r, carry):
            mixed = None
            for i in range(len(lses)):
                term = to_column(share[i, pl.ds(r, 1), :], queries) * read(i, r).astype(F32)
                mixed = term if mixed is None else mixed + term
            write(r, mixed)
            return carry

        lax.fori_loop(0, rows, one_row, 0, unroll=4)
        return peak + jnp.log2(total)

    for k in order:
        own = lax.rem(a + k, outer) * inner + b
        for j in range(1, inner):
            for copy in side_copies(k, j):
                copy.wait_recv()

        def read(i, r, k=k, own=own):
            return o_ref[own, r] if i == 0 else side_o[k, i, r]

        def write(r, mixed, k=k):
            pass_o[k, r] = mixed.astype(BF16)

        lses = [lse_ref[own]] + [side_l[k, j] for j in range(1, inner)]
        pass_l[k] = blend(lses, read, write)
        if k:
            for copy in line_copies(k):
                copy.start()
                sent.append(copy)
    for k in range(1, outer):
        for copy in line_copies(k):
            copy.wait_recv()

    def read(i, r):
        if i == outer:
            return s_ref[r]
        return pass_o[0, r] if i == 0 else line_o[i, r]

    group = queries // (kv * steps)

    def write(r, mixed):
        for c in range(kv):
            for t in range(steps):
                first = pl.multiple_of((r * steps + t) * (kv * group) + c * group, group)
                at = (c * steps + t) * group
                flat[pl.ds(first, group), :] = mixed[at:at + group]

    blend([pass_l[0]] + [line_l[k] for k in range(1, outer)] + [s_lse[...]], read, write)
    heads = kv * group
    for h in range(heads):
        att_all[me, :, h * width:(h + 1) * width] = flat[pl.ds(h, rows * steps, stride=heads), :].astype(BF16)
    gather = Gather(n, me, [att_all], gs1, gr1, gs2, gr2)
    gather.start()

    vocab, (_, token_rows) = vocab_own, tokens_ref.shape
    first_id = head * vocab
    each = 16 // steps
    lane = lax.broadcasted_iota(jnp.int32, (16, 256), 1)
    owner = lane // 16 == lax.broadcasted_iota(jnp.int32, (16, 256), 0)
    fetch.wait()

    def pick(i, carry):
        wanted = jnp.full((16, 256), -1, jnp.int32)
        for x in range(16):
            token = tokens_ref[x % steps, i * each + x // steps] - first_id
            inside = jnp.logical_and(token >= 0, token < vocab)
            wanted = jnp.where(lane // 16 == x, jnp.where(inside, lax.rem(token, 16), -1), wanted)
        chosen = jnp.logical_and(owner, lax.rem(lane, 16) == wanted).astype(F32).astype(BF16)
        block = block_buf[pl.ds(pl.multiple_of(i * 256, 256), 256), :]
        e_buf[pl.ds(pl.multiple_of(i * 16, 16), 16), :] = jnp.dot(chosen, block, preferred_element_type=F32)
        return carry

    groups = token_rows * steps // 16
    for k in range(1, outer):
        lax.fori_loop(groups * (k - 1) // outer, groups * k // outer, pick, 0)
        gather.forward(k)
    lax.fori_loop(groups * (outer - 1) // outer, groups, pick, 0)
    load.wait()

    columns = part.shape[2]
    tile = min(256, columns)
    chunk = rows * steps
    span = n // heads_n

    def project(j, cols):
        where = lax.rem(b + j, inner)
        lhs = jnp.concatenate([att_all[x * inner + where] for x in range(outer)], axis=0)
        done = jnp.dot(lhs, w_buf[:, cols], preferred_element_type=F32)
        for x in range(outer):
            shard = x * inner + where
            at = pl.ds(pl.multiple_of(shard * chunk, chunk), chunk)
            part[shard, :, cols] = (done[x * chunk:(x + 1) * chunk] + e_buf[at, cols]).astype(BF16)

    def head_copy(i, q, cols):
        peer = lax.rem(head + i, heads_n)
        return remote(part.at[pl.ds(peer * span, span), :, cols], landed.at[i, :, :, cols], hs.at[i, q], hr.at[i, q], head=peer)

    cuts = [slice(x, x + tile) for x in range(0, columns, tile)]
    for cols in cuts:
        project(0, cols)
    gather.finish()
    for q, cols in enumerate(cuts):
        for j in range(1, inner):
            project(j, cols)
        for i in range(1, heads_n):
            copy = head_copy(i, q, cols)
            copy.start()
            sent.append(copy)
    for q, cols in enumerate(cuts):
        for i in range(1, heads_n):
            head_copy(i, q, cols).wait_recv()
        total = part[pl.ds(head * span, span), :, cols].astype(F32)
        for i in range(1, heads_n):
            total = total + landed[i, :, :, cols].astype(F32)
        out_ref[:, :, cols] = total.astype(BF16).reshape(out_ref.shape[:2] + (tile,))
    for copy in sent:
        copy.wait_send()


def smem():
    return pl.BlockSpec(memory_space=pltpu.SMEM)


def vmem():
    return pl.BlockSpec(memory_space=pltpu.VMEM)


def shards(n, heads_n, queries, new_kv, prompt_keys, prompt_values, suffix_kv, prompt_ids, suffix_lengths,
           token_ids, embedding, out_weight):
    steps, rows, heads, width = queries.shape
    prompts, positions, kv, _ = prompt_keys.shape
    group = heads // kv
    per = steps * group
    suf = suffix_kv.shape[2]
    all_rows = n * rows
    outer, inner = split_axis(n)
    scale2 = width ** -0.5 * math.log2(math.e)
    sds = jax.ShapeDtypeStruct
    dma = pltpu.SemaphoreType.DMA

    q_own = queries.reshape(steps, rows, kv, group, width).transpose(1, 2, 0, 3, 4).reshape(rows, kv, per, width)
    live = suf + 128
    q_all, ids_all, s_mixed, s_lse = pl.pallas_call(
        functools.partial(share_kernel, n, scale2, steps),
        out_shape=(sds((n, rows, kv, per, width), BF16), sds((n, rows, 128), jnp.int32),
                   sds((rows, kv * per, width), F32), sds((rows, 128), F32)),
        in_specs=[smem(), smem(), vmem(), vmem(), pl.BlockSpec(memory_space=pl.ANY)],
        out_specs=(vmem(),) * 4,
        scratch_shapes=[
            pltpu.VMEM((2, rows, suf * kv, width), BF16), pltpu.VMEM((2, suf * kv, width), F32),
            pltpu.VMEM((kv, live, width), BF16), pltpu.VMEM((kv, live, width), BF16), dma((1,)),
            *gather_sems(n, 2)],
        compiler_params=pltpu.CompilerParams(collective_id=0, has_side_effects=True, vmem_limit_bytes=VMEM_BYTES),
        name="share_queries",
    )(suffix_lengths.astype(jnp.int32), prompt_ids.astype(jnp.int32).T, q_own, new_kv, suffix_kv.reshape(2, rows, suf * kv, width))

    tokens = all_rows * steps
    vocab = embedding.shape[0]
    tile = 4
    fixed = lambda *shape: pl.BlockSpec(shape, lambda p, *_: (0,) * len(shape))
    cut = pl.BlockSpec((1, positions * kv, width), lambda p, *_: (p, 0, 0))
    o_all, lse_all, blocks = pl.pallas_call(
        functools.partial(prompt_kernel, scale2, tile),
        out_shape=(sds((all_rows, kv * per, width), BF16), sds((all_rows, 128), F32), sds((tokens * 16, embedding.shape[1]), BF16)),
        grid=(prompts,),
        in_specs=[smem(), smem(), fixed(all_rows, kv, per, width), cut, cut, pl.BlockSpec(memory_space=pl.ANY)],
        out_specs=(fixed(all_rows, kv * per, width), fixed(all_rows, 128), pl.BlockSpec(memory_space=pl.ANY)),
        scratch_shapes=[
            pltpu.SMEM((prompts * (all_rows + tile),), jnp.int32), pltpu.SMEM((prompts,), jnp.int32),
            pltpu.VMEM((2, positions * kv, width), F32),
            pltpu.VMEM((kv, positions, width), BF16), pltpu.VMEM((kv, positions, 2 * width), BF16),
            pltpu.VMEM((tokens * 16, embedding.shape[1]), BF16), dma((2,))],
        compiler_params=pltpu.CompilerParams(vmem_limit_bytes=VMEM_BYTES),
        name="prompt_attention",
    )(token_ids.T, ids_all.reshape(all_rows, 128), q_all.reshape(all_rows, kv, per, width),
      prompt_keys.reshape(prompts, positions * kv, width), prompt_values.reshape(prompts, positions * kv, width), embedding)

    columns = out_weight.shape[1]
    pair = dma((outer, inner))
    out = pl.pallas_call(
        functools.partial(finish_kernel, n, heads_n, steps, kv, embedding.shape[0]),
        out_shape=sds((all_rows // heads_n, steps, columns), BF16),
        in_specs=[vmem()] * 4 + [smem()] + [pl.BlockSpec(memory_space=pl.ANY)] * 2,
        out_specs=vmem(),
        scratch_shapes=[
            pltpu.VMEM((outer, inner, rows, kv * per, width), BF16), pltpu.VMEM((outer, inner, rows, 128), F32),
            pltpu.VMEM((outer, rows, kv * per, width), BF16), pltpu.VMEM((outer, rows, 128), F32),
            pltpu.VMEM((outer, rows, kv * per, width), BF16), pltpu.VMEM((outer, rows, 128), F32),
            pltpu.VMEM((max(inner, outer + 1), rows, 128), F32), pltpu.VMEM((rows * kv * per, width), F32),
            pltpu.VMEM((n, rows * steps, heads * width), BF16), pltpu.VMEM(out_weight.shape, BF16),
            pltpu.VMEM((tokens, columns), F32), pltpu.VMEM(blocks.shape, BF16),
            pltpu.VMEM((n, rows * steps, columns), BF16), pltpu.VMEM((heads_n, n // heads_n, rows * steps, columns), BF16),
            dma((2,)), pair, pair, pair, pair, dma((outer,)), dma((outer,)), dma((outer,)), dma((outer,)),
            *gather_sems(n, 1), dma((heads_n, 8)), dma((heads_n, 8))],
        compiler_params=pltpu.CompilerParams(collective_id=1, has_side_effects=True, vmem_limit_bytes=VMEM_BYTES),
        name="finish",
    )(o_all.reshape(n, rows, kv * per, width), lse_all.reshape(n, rows, 128), s_mixed, s_lse, token_ids.T, out_weight, blocks)
    return out


def solution(mesh):
    return jax.shard_map(
        functools.partial(shards, mesh.shape["seq"], mesh.shape["head"]),
        mesh=mesh,
        in_specs=(
            P(None, "seq", "head", None),
            P(None, None, "seq", "head", None),
            P(None, "seq", "head", None),
            P(None, "seq", "head", None),
            P(None, "seq", None, "head", None),
            P("seq", None),
            P("seq"),
            P(),
            P("head", "seq"),
            P("head", "seq"),
        ),
        out_specs=P("head", None, "seq"),
        check_vma=False,
    )
```
